32 devices in a mesh: shard: 4 (over y, x), ctx: 4 (over z), tensor: 2 (over core).
Axes of the slice: x: 2, y: 2, z: 4, core: 2. Of those that a mesh axis runs over, the one named last changes fastest.
Arguments:
- tokens: bfloat16 [16, 1024, 768], P('shard', 'ctx'), may hold values from -6 to 6
- gain_in: float32 [768], replicated, may hold values from 0.5 to 1.5
- w_z: bfloat16 [768, 1536], P('shard', 'tensor'), may hold values from -0.21875 to 0.21875
- w_x: bfloat16 [768, 1536], P('shard', 'tensor'), may hold values from -0.21875 to 0.21875
- w_bc: bfloat16 [768, 256], P('shard'), may hold values from -0.21875 to 0.21875
- w_dt: bfloat16 [768, 24], P('shard', 'tensor'), may hold values from -0.21875 to 0.21875
- conv_x: float32 [4, 1536], P(None, 'tensor'), may hold values from -3 to 3
- conv_bc: float32 [4, 256], replicated, may hold values from -3 to 3
- bias_x: float32 [1536], P('tensor'), may hold values from -2 to 2
- bias_bc: float32 [256], replicated, may hold values from -2 to 2
- dt_bias: float32 [24], P('tensor'), may hold values from -6 to -2.5
- a_log: float32 [24], P('tensor'), may hold values from -3.5 to 2
- d_skip: float32 [24], P('tensor'), may hold values from 0.5 to 2
- gain_out: float32 [1536], P('tensor'), may hold values from 0.5 to 1.5
- w_out: bfloat16 [1536, 768], P('tensor', 'shard'), may hold values from -0.15625 to 0.15625
- cotangent: bfloat16 [16, 1024, 768], P('shard', 'ctx'), may hold values from -6 to 6
Outputs:
- block_out: bfloat16 [16, 1024, 768], P('shard', 'ctx')
- grad_tokens: float32 [16, 1024, 768], P('shard', 'ctx')
- grad_gain_in: float32 [768], replicated
- grad_w_z: float32 [768, 1536], P('shard', 'tensor')
- grad_w_x: float32 [768, 1536], P('shard', 'tensor')
- grad_w_bc: float32 [768, 256], P('shard')
- grad_w_dt: float32 [768, 24], P('shard', 'tensor')
- grad_conv_x: float32 [4, 1536], P(None, 'tensor')
- grad_conv_bc: float32 [4, 256], replicated
- grad_bias_x: float32 [1536], P('tensor')
- grad_bias_bc: float32 [256], replicated
- grad_dt_bias: float32 [24], P('tensor')
- grad_a_log: float32 [24], P('tensor')
- grad_d_skip: float32 [24], P('tensor')
- grad_gain_out: float32 [1536], P('tensor')
- grad_w_out: float32 [1536, 768], P('tensor', 'shard')
The draws below stay inside these ranges and needn't reach their ends.
All inputs are finite; a program needn't handle non-finite values.
Results may differ from the reference program's by a relative error of at most 0.0085.
Values may be sent and summed in bfloat16 or wider, within the bound.
A program may use at most 128 MiB of HBM per device.

```python
from functools import partial
import jax
import jax.numpy as jnp
from jax import lax

D = 768
H = 24
N = 128
CONV = 4
GROUP = 256
E = 1536
LEN = 1024
SEQS = 16


def steps_of(own_key, extent, split, low, largest):
    def one(dim, parts):
        heights = jax.random.uniform(jax.random.fold_in(jax.random.fold_in(own_key, 6), dim), (parts,), jnp.float32, low / len(split), largest / len(split))
        return jnp.repeat(jnp.exp(heights), extent[dim] // parts).reshape((-1,) + (1,) * (len(extent) - dim - 1))

    gain = one(*split[0])
    for cut in split[1:]:
        gain = gain * one(*cut)
    return gain


def noise(rng, extent, scale, limit, shards=(), dtype=jnp.bfloat16):
    values = jax.random.normal(rng, extent, jnp.float32) * scale
    if len(shards) > 0:
        values = steps_of(rng, extent, shards, -0.22, 0.18) * values
    return jnp.clip(values, min=-limit, max=limit).astype(dtype)


def setup_inputs(seed: int = 0) -> dict:
    arg_keys = jax.random.split(jax.random.key(seed), 17)
    tokens = noise(arg_keys[0], (SEQS, LEN, D), 1.0, 6.0, ((0, 4), (1, 4)))
    gain_in = jnp.clip(1.0 + 0.1 * jax.random.normal(arg_keys[1], (D,), jnp.float32), 0.5, 1.5)
    w_z = noise(arg_keys[2], (D, E), D ** -0.5, 0.21875, ((0, 4), (1, 2)))
    w_x = noise(arg_keys[3], (D, E), D ** -0.5, 0.21875, ((0, 4), (1, 2)))
    w_bc = noise(arg_keys[4], (D, 2 * N), D ** -0.5, 0.21875, ((0, 4),))
    w_dt = noise(arg_keys[5], (D, H), D ** -0.5, 0.21875, ((0, 4), (1, 2)))
    conv_x = noise(arg_keys[6], (CONV, E), CONV ** -0.5, 3.0, ((1, 2),), jnp.float32)
    conv_bc = noise(arg_keys[7], (CONV, 2 * N), CONV ** -0.5, 3.0, (), jnp.float32)
    bias_x = noise(arg_keys[8], (E,), 0.3, 2.0, ((0, 2),), jnp.float32)
    bias_bc = noise(arg_keys[9], (2 * N,), 0.3, 2.0, (), jnp.float32)
    dt_bias = jnp.clip(-6.0 + 3.5 * jax.random.uniform(arg_keys[10], (H,), jnp.float32) ** steps_of(arg_keys[10], (H,), ((0, 2),), -0.2, 0.2), -6.0, -2.5)
    a_log = jnp.clip(-3.5 + 5.5 * jax.random.uniform(arg_keys[11], (H,), jnp.float32) ** steps_of(arg_keys[11], (H,), ((0, 2),), -0.2, 0.2), -3.5, 2.0)
    d_skip = jnp.clip(0.5 + 1.5 * jax.random.uniform(arg_keys[12], (H,), jnp.float32) ** steps_of(arg_keys[12], (H,), ((0, 2),), -0.2, 0.2), 0.5, 2.0)
    gain_out = jnp.clip(1.0 + 0.1 * jax.random.normal(arg_keys[13], (E,), jnp.float32), 0.5, 1.5)
    w_out = noise(arg_keys[14], (E, D), E ** -0.5, 0.15625, ((0, 2), (1, 4)))
    cotangent = noise(arg_keys[15], (SEQS, LEN, D), 1.0, 6.0, ((0, 4), (1, 4)))
    return dict(tokens=tokens, gain_in=gain_in, w_z=w_z, w_x=w_x, w_bc=w_bc, w_dt=w_dt, conv_x=conv_x, conv_bc=conv_bc, bias_x=bias_x, bias_bc=bias_bc, dt_bias=dt_bias, a_log=a_log, d_skip=d_skip, gain_out=gain_out, w_out=w_out, cotangent=cotangent)


@jax.custom_vjp
def low(v):
    return lax.optimization_barrier(v.astype(jnp.bfloat16)).astype(jnp.float32)

@jax.custom_vjp
def low_back(v):
    return v

def low_keep(v):
    return (low(v), None)

def low_pass(kept, grad):
    return (grad,)

def back_keep(v):
    return (v, None)

def back_low(kept, grad):
    return (low(grad),)
low.defvjp(low_keep, low_pass)
low_back.defvjp(back_keep, back_low)
highest = lax.Precision.HIGHEST
epsilon = 1e-05

def causal_mix(raw, weight, bias):
    taps = weight.shape[0]
    length = raw.shape[0]
    padded = jnp.concatenate([jnp.zeros((taps - 1, raw.shape[1]), jnp.float32), raw], axis=0)
    total = bias[None, :] + jnp.zeros_like(raw)
    for offset in range(taps):
        total = total + weight[offset][None, :] * padded[offset:offset + length]
    return jax.nn.silu(total)

def group_step(d_skip, state, pieces):
    values, bc_rows, step_size, log_decay = pieces
    half = bc_rows.shape[1] // 2
    b_rows = bc_rows[:, :half]
    c_rows = bc_rows[:, half:]
    length = values.shape[0]
    cum = jnp.cumsum(log_decay, axis=0)
    cum_t = cum.T
    spread = cum_t[:, :, None] - cum_t[:, None, :]
    lower = jnp.arange(length)[:, None] >= jnp.arange(length)[None, :]
    decay = jnp.exp(jnp.where(lower[None], spread, -1e+30))
    intersection = jnp.dot(c_rows, b_rows.T, precision=highest, preferred_element_type=jnp.float32)
    mixing = intersection[None] * decay * step_size.T[:, None, :]
    inner = jnp.einsum('htu,uhp->thp', mixing, values, precision=highest)
    outer = jnp.einsum('tn,hpn->thp', c_rows, state, precision=highest) * jnp.exp(cum)[:, :, None]
    mixed = inner + outer + d_skip[None, :, None] * values
    weights = jnp.exp(cum[-1:, :] - cum) * step_size
    own_state = jnp.einsum('lh,lhp,ln->hpn', weights, values, b_rows, precision=highest)
    new_state = jnp.exp(cum[-1])[:, None, None] * state + own_state
    return (new_state, mixed)

def forward(tokens, gain_in, w_z, w_x, w_bc, w_dt, conv_x, conv_bc, bias_x, bias_bc, dt_bias, a_log, d_skip, gain_out, w_out):
    length, width = tokens.shape
    heads = dt_bias.shape[0]
    inner_units = w_x.shape[1]
    head_dim = inner_units // heads
    state_dim = w_bc.shape[1] // 2
    inv_rms = lax.rsqrt(lax.optimization_barrier(jnp.mean(tokens * tokens, axis=-1, keepdims=True)) + epsilon)
    normed = low(tokens * inv_rms * gain_in[None, :])
    weight = jnp.concatenate([w_z, w_x, w_bc, w_dt], axis=1)
    proj = low_back(jnp.dot(normed, weight, precision=highest, preferred_element_type=jnp.float32))
    z_part = proj[:, :inner_units]
    x_part = proj[:, inner_units:2 * inner_units]
    bc_part = proj[:, 2 * inner_units:2 * inner_units + 2 * state_dim]
    dt_part = proj[:, 2 * inner_units + 2 * state_dim:]
    values = causal_mix(x_part, conv_x, bias_x)
    bc_rows = causal_mix(bc_part, conv_bc, bias_bc)
    step_size = jax.nn.softplus(dt_part + dt_bias[None, :])
    log_decay = -step_size * jnp.exp(a_log)[None, :]
    blocks = length // GROUP
    pieces = (values.reshape(blocks, GROUP, heads, head_dim), bc_rows.reshape(blocks, GROUP, 2 * state_dim), step_size.reshape(blocks, GROUP, heads), log_decay.reshape(blocks, GROUP, heads))
    start = jnp.zeros((heads, head_dim, state_dim), jnp.float32)
    final_state, mixed = lax.scan(jax.checkpoint(partial(group_step, d_skip)), start, pieces)
    mixed = mixed.reshape(length, inner_units)
    gated = mixed * jax.nn.silu(z_part)
    inv_gate = lax.rsqrt(lax.optimization_barrier(jnp.mean(gated * gated, axis=-1, keepdims=True)) + epsilon)
    gated_norm = low(gated * inv_gate * gain_out[None, :])
    out = jnp.dot(gated_norm, w_out, precision=highest, preferred_element_type=jnp.float32)
    return tokens + out

def reference(tokens, gain_in, w_z, w_x, w_bc, w_dt, conv_x, conv_bc, bias_x, bias_bc, dt_bias, a_log, d_skip, gain_out, w_out, cotangent):
    params = tuple((param.astype(jnp.float32) for param in (gain_in, w_z, w_x, w_bc, w_dt, conv_x, conv_bc, bias_x, bias_bc, dt_bias, a_log, d_skip, gain_out, w_out)))

    def one_sequence(totals, pair):
        seq_tokens, seq_cot = pair
        result, back = jax.vjp(forward, seq_tokens.astype(jnp.float32), *params)
        grads = back(seq_cot.astype(jnp.float32))
        totals = tuple((total + grad for total, grad in zip(totals, grads[1:])))
        return (totals, (result.astype(jnp.bfloat16), grads[0]))
    zeros = tuple((jnp.zeros_like(param) for param in params))
    totals, outputs = lax.scan(one_sequence, zeros, (tokens, cotangent))
    block_out, grad_tokens = outputs
    return (block_out, grad_tokens, totals[0], totals[1], totals[2], totals[3], totals[4], totals[5], totals[6], totals[7], totals[8], totals[9], totals[10], totals[11], totals[12], totals[13])
```

```python
import functools

import jax
import jax.numpy as jnp
from jax import lax
from jax.experimental import pallas as pl
from jax.experimental.pallas import tpu as pltpu
from jax.sharding import PartitionSpec as P

highest = lax.Precision.HIGH
epsilon = 1e-05
lanes = 128


def sum_pair(part, low):
    if lax.axis_size("tensor") != 2:
        return lax.psum(part, "tensor")
    if low:
        own = lax.reduce_precision(part, 8, 7)
        other = lax.ppermute(own.astype(jnp.bfloat16), "tensor", [(0, 1), (1, 0)])
        return own + other.astype(jnp.float32)
    return part + lax.ppermute(part, "tensor", [(0, 1), (1, 0)])


def reduce_kernel(
    n_shard, n_ctx, groups, g_ref, out_ref, first, send, second, low, third, sems
):
    shard, ctx = lax.axis_index("shard"), lax.axis_index("ctx")
    rows = out_ref.shape[0]
    cols = n_ctx * lanes
    shard_peers = [lax.rem(shard + d, n_shard) for d in range(1, n_shard)]
    ctx_peers = [lax.rem(ctx + d, n_ctx) for d in range(1, n_ctx)]
    senders = [lax.rem(ctx + n_ctx - d, n_ctx) for d in range(1, n_ctx)]
    barrier = pltpu.get_barrier_semaphore()
    for peer in shard_peers:
        pl.semaphore_signal(
            barrier, inc=1, device_id={"shard": peer}, device_id_type=pl.DeviceIdType.MESH
        )
    for peer in ctx_peers:
        pl.semaphore_signal(
            barrier, inc=1, device_id={"ctx": peer}, device_id_type=pl.DeviceIdType.MESH
        )
    pl.semaphore_wait(barrier, n_shard + n_ctx - 2)

    def copy(source, target, send_sem, recv_sem, place):
        return pltpu.make_async_remote_copy(
            src_ref=source,
            dst_ref=target,
            send_sem=send_sem,
            recv_sem=recv_sem,
            device_id=place,
            device_id_type=pl.DeviceIdType.MESH,
        )

    s1s, s1r, s2s, s2r, s3s, s3r = sems
    started = []
    one, two, three = {}, {}, {}
    for g in range(groups):
        for i, peer in enumerate(shard_peers):
            part = g_ref.at[pl.ds(pl.multiple_of(peer * rows, 16), rows), pl.ds(g * cols, cols)]
            one[g, i] = copy(part, first.at[g, i], s1s.at[g, i], s1r.at[g, i], {"shard": peer})
            one[g, i].start()

    def scatter(g):
        total = g_ref[
            pl.ds(pl.multiple_of(shard * rows, 16), rows), pl.ds(g * cols, cols)
        ].astype(jnp.float32)
        for i in range(n_shard - 1):
            one[g, i].wait_recv()
            total = total + first[g, i].astype(jnp.float32)
        for j in range(n_ctx):
            send[g, j] = total[:, j * lanes : (j + 1) * lanes].astype(jnp.bfloat16)
        for i, peer in enumerate(ctx_peers):
            two[g, i] = copy(
                send.at[g, peer], second.at[g, i], s2s.at[g, i], s2r.at[g, i], {"ctx": peer}
            )
            two[g, i].start()

    def gather(g):
        total = send[g, ctx].astype(jnp.float32)
        for i in range(n_ctx - 1):
            two[g, i].wait_recv()
            total = total + second[g, i].astype(jnp.float32)
        low[g] = total.astype(jnp.bfloat16)
        for i, peer in enumerate(ctx_peers):
            three[g, i] = copy(
                low.at[g], third.at[g, i], s3s.at[g, i], s3r.at[g, i], {"ctx": peer}
            )
            three[g, i].start()
        out_ref[:, pl.ds(pl.multiple_of(g * cols + ctx * lanes, lanes), lanes)] = low[g].astype(
            jnp.float32
        )

    def finish(g):
        for i, sender in enumerate(senders):
            three[g, i].wait_recv()
            out_ref[:, pl.ds(pl.multiple_of(g * cols + sender * lanes, lanes), lanes)] = third[
                g, i
            ].astype(jnp.float32)

    for g in range(groups + 2):
        if g < groups:
            scatter(g)
        if 0 <= g - 1 < groups:
            gather(g - 1)
        if 0 <= g - 2 < groups:
            finish(g - 2)
    for copies in (one, two, three):
        for each in copies.values():
            each.wait_send()


def reduce_to_owners(parts):
    n_shard, n_ctx = lax.axis_size("shard"), lax.axis_size("ctx")
    together = jnp.concatenate(parts, axis=1)
    height, wide = together.shape
    cols = n_ctx * lanes
    groups = -(-wide // cols)
    if groups * cols > wide:
        together = jnp.pad(together, ((0, 0), (0, groups * cols - wide)))
    rows = height // n_shard
    dma = pltpu.SemaphoreType.DMA
    return pl.pallas_call(
        functools.partial(reduce_kernel, n_shard, n_ctx, groups),
        out_shape=jax.ShapeDtypeStruct((rows, groups * cols), jnp.float32),
        in_specs=[pl.BlockSpec(memory_space=pltpu.VMEM)],
        out_specs=pl.BlockSpec(memory_space=pltpu.VMEM),
        scratch_shapes=[
            pltpu.VMEM((groups, n_shard - 1, rows, cols), jnp.bfloat16),
            pltpu.VMEM((groups, n_ctx, rows, lanes), jnp.bfloat16),
            pltpu.VMEM((groups, n_ctx - 1, rows, lanes), jnp.bfloat16),
            pltpu.VMEM((groups, rows, lanes), jnp.bfloat16),
            pltpu.VMEM((groups, n_ctx - 1, rows, lanes), jnp.bfloat16),
            [
                dma((groups, n_shard - 1)),
                dma((groups, n_shard - 1)),
                dma((groups, n_ctx - 1)),
                dma((groups, n_ctx - 1)),
                dma((groups, n_ctx - 1)),
                dma((groups, n_ctx - 1)),
            ],
        ],
        compiler_params=pltpu.CompilerParams(
            collective_id=0, has_side_effects=True, vmem_limit_bytes=40 * 1024 * 1024
        ),
    )(together)


def passed_along(block, axis, distance):
    devices = range(lax.axis_size(axis))
    route = [(i - distance, i) for i in devices if i - distance in devices]
    return lax.ppermute(block, axis, route)


def carried_in(part, axis, combine, identity, reverse):
    count = lax.axis_size(axis)
    place = lax.axis_index(axis)
    ahead = count - 1 - place if reverse else place
    gathered = (
        lax.all_gather(part[0], axis),
        lax.all_gather(part[1].astype(jnp.bfloat16), axis),
    )
    state = jax.tree.map(lambda a, e: jnp.zeros_like(a) + jnp.asarray(e, a.dtype), part, identity)

    def one(step, state):
        source = count - 1 - step if reverse else step
        return combine(
            state,
            jax.tree.map(
                lambda a: lax.dynamic_index_in_dim(a, source, 0, False).astype(jnp.float32),
                gathered,
            )
        )

    return lax.fori_loop(0, ahead, one, state)


def low_dot(left, right):
    return jnp.dot(left, right, preferred_element_type=jnp.float32)


def dot_right(left, right):
    return lax.dot_general(
        left, right, (((1,), (1,)), ((), ())), preferred_element_type=jnp.float32
    )


def dot_left(left, right):
    return lax.dot_general(
        left, right, (((0,), (0,)), ((), ())), preferred_element_type=jnp.float32
    )


def causal_mix(raw, edge, weight, bias):
    length = raw.shape[1]
    padded = jnp.concatenate([edge, raw], axis=1)
    total = bias[None, None, :] + jnp.zeros_like(raw)
    for offset in range(weight.shape[0]):
        total = total + weight[offset][None, None, :] * padded[:, offset : offset + length]
    return jax.nn.silu(total)


def prepare(
    x_part, bc_part, dt_part, edge_x, edge_bc, conv_x, conv_bc, bias_x, bias_bc, dt_bias, a_log
):
    values = causal_mix(x_part, edge_x, conv_x, bias_x)
    bc_rows = causal_mix(bc_part, edge_bc, conv_bc, bias_bc)
    step_size = jax.nn.softplus(dt_part + dt_bias[None, None, :])
    log_decay = -step_size * jnp.exp(a_log)[None, None, :]
    return (values, bc_rows, step_size, log_decay)


def local_state(values, bc_rows, step_size, cum):
    seq_count, length, heads = step_size.shape
    half = bc_rows.shape[-1] // 2
    values_four = values.reshape(seq_count, length, heads, -1)
    weights = jnp.exp(cum[:, -1:, :] - cum) * step_size
    return jnp.einsum(
        "slh,slhp,sln->shpn", weights, values_four, bc_rows[..., :half], precision=highest
    )


def combine_carry(earlier, later):
    return (earlier[0] * later[0], later[1] + later[0][..., None, None] * earlier[1])


def mixer(values, bc_rows, step_size, log_decay, z_part, d_skip, prev_state):
    seq_count, length, heads = step_size.shape
    half = bc_rows.shape[-1] // 2
    values_four = values.reshape(seq_count, length, heads, -1)
    b_rows = bc_rows[..., :half]
    c_rows = bc_rows[..., half:]
    cum = jnp.cumsum(log_decay, axis=1)
    cum_t = jnp.swapaxes(cum, 1, 2)
    spread = cum_t[..., :, None] - cum_t[..., None, :]
    lower = jnp.arange(length)[:, None] >= jnp.arange(length)[None, :]
    decay = jnp.exp(jnp.where(lower[None, None], spread, -1e30))
    intersection = jnp.einsum("stn,sun->stu", c_rows, b_rows, precision=highest)
    mixing = intersection[:, None] * decay * jnp.swapaxes(step_size, 1, 2)[:, :, None, :]
    inner = jnp.einsum("shtu,suhp->sthp", mixing, values_four, precision=highest)
    outer = (
        jnp.einsum("stn,shpn->sthp", c_rows, prev_state, precision=highest)
        * jnp.exp(cum)[..., None]
    )
    mixed = inner + outer + d_skip[None, None, :, None] * values_four
    gated = mixed.reshape(seq_count, length, -1) * jax.nn.silu(z_part)
    end_state = jnp.exp(cum[:, -1])[..., None, None] * prev_state + local_state(
        values, bc_rows, step_size, cum
    )
    return (gated, end_state)


def shards(
    tokens,
    gain_in,
    w_z,
    w_x,
    w_bc,
    w_dt,
    conv_x,
    conv_bc,
    bias_x,
    bias_bc,
    dt_bias,
    a_log,
    d_skip,
    gain_out,
    w_out,
    cotangent,
):
    seq_count, row_count, width = tokens.shape
    flat_count = seq_count * row_count
    tokens_f = tokens.astype(jnp.float32)
    inv_rms = lax.rsqrt(jnp.mean(tokens_f * tokens_f, axis=-1, keepdims=True) + epsilon)
    normed = (
        (tokens_f * inv_rms * gain_in[None, None, :])
        .astype(jnp.bfloat16)
        .reshape(flat_count, width)
    )
    x_units, bc_units = w_x.shape[1], w_bc.shape[1]
    full_xbd = lax.all_gather(
        jnp.concatenate([w_x, w_bc, w_dt], axis=1), "shard", axis=0, tiled=True
    )
    full_z = lax.all_gather(w_z, "shard", axis=0, tiled=True)
    full_out = lax.all_gather(w_out.T, "shard", axis=0, tiled=True).T
    full_x = full_xbd[:, :x_units]
    full_bc = full_xbd[:, x_units : x_units + bc_units]
    full_dt = full_xbd[:, x_units + bc_units :]
    z_part = low_dot(normed, full_z).reshape(seq_count, row_count, -1)
    xbd_part = low_dot(normed, full_xbd).reshape(seq_count, row_count, -1)
    x_part = xbd_part[..., :x_units]
    bc_part = xbd_part[..., x_units : x_units + bc_units]
    dt_part = xbd_part[..., x_units + bc_units :]
    rim = conv_x.shape[0] - 1
    edge_x, edge_bc = passed_along(
        (x_part[:, row_count - rim :], bc_part[:, row_count - rim :]), "ctx", 1
    )
    prepared, prep_back = jax.vjp(
        prepare,
        x_part,
        bc_part,
        dt_part,
        edge_x,
        edge_bc,
        conv_x,
        conv_bc,
        bias_x,
        bias_bc,
        dt_bias,
        a_log,
    )
    values, bc_rows, step_size, log_decay = prepared
    cum = jnp.cumsum(log_decay, axis=1)
    carry_gain = jnp.exp(cum[:, -1])
    own_state = local_state(values, bc_rows, step_size, cum)
    identity = (jnp.ones_like(carry_gain), jnp.zeros_like(own_state))
    gain_before, prev_state = carried_in(
        (carry_gain, own_state), "ctx", combine_carry, identity, False
    )
    mixer_out, mixer_back = jax.vjp(
        mixer, values, bc_rows, step_size, log_decay, z_part, d_skip, prev_state
    )
    gated = mixer_out[0]
    inner_total = gated.shape[-1] * lax.axis_size("tensor")
    squares = sum_pair(jnp.sum(gated * gated, axis=-1), False)
    inv_gate = lax.rsqrt(squares / inner_total + epsilon)[..., None]
    gated_low = (
        (gated * inv_gate * gain_out[None, None, :]).astype(jnp.bfloat16).reshape(flat_count, -1)
    )
    partial_out = low_dot(gated_low, full_out)
    total_out = sum_pair(partial_out, True)
    block_out = (tokens_f + total_out.reshape(seq_count, row_count, width)).astype(jnp.bfloat16)
    cot_flat = cotangent.reshape(flat_count, width)
    grad_w_out = dot_left(cot_flat, gated_low)
    d_norm = dot_right(cot_flat, full_out).reshape(seq_count, row_count, -1)
    grad_gain_out = jnp.sum(d_norm * gated * inv_gate, axis=(0, 1))
    scaled = d_norm * gain_out[None, None, :]
    inner_prod = sum_pair(jnp.sum(scaled * gated, axis=-1), False)[..., None]
    d_gated = inv_gate * scaled - gated * inv_gate**3 * inner_prod / inner_total
    half = bc_rows.shape[-1] // 2
    heads = step_size.shape[-1]
    d_mixed = (d_gated * jax.nn.silu(z_part)).reshape(seq_count, row_count, heads, -1)
    local_grad = jnp.einsum(
        "sthp,stn->shpn", d_mixed * jnp.exp(cum)[..., None], bc_rows[..., half:], precision=highest
    )
    gain_after, after_grad = carried_in(
        (carry_gain, local_grad), "ctx", combine_carry, identity, True
    )
    mixer_grads = mixer_back((d_gated, after_grad))
    d_values, d_bc, d_step, d_decay, d_z, grad_d_skip = mixer_grads[:6]
    d_bc_total = sum_pair(d_bc, False)
    prep_grads = prep_back((d_values, d_bc_total, d_step, d_decay))
    d_x_part, d_bc_part, d_dt_part, d_edge_x, d_edge_bc = prep_grads[:5]
    grad_conv_x, grad_conv_bc, grad_bias_x, grad_bias_bc, grad_dt_bias, grad_a_log = prep_grads[5:]
    back_x, back_bc = (
        passed_along(d_edge_x.astype(jnp.bfloat16), "ctx", -1).astype(d_edge_x.dtype),
        passed_along(d_edge_bc.astype(jnp.bfloat16), "ctx", -1).astype(d_edge_bc.dtype),
    )
    d_x_part = d_x_part + jnp.pad(back_x, ((0, 0), (row_count - rim, 0), (0, 0)))
    d_bc_part = d_bc_part + jnp.pad(back_bc, ((0, 0), (row_count - rim, 0), (0, 0)))
    low_z = d_z.astype(jnp.bfloat16).reshape(flat_count, -1)
    low_x = d_x_part.astype(jnp.bfloat16).reshape(flat_count, -1)
    low_bc = d_bc_part.astype(jnp.bfloat16).reshape(flat_count, -1)
    low_dt = d_dt_part.astype(jnp.bfloat16).reshape(flat_count, -1)
    part_in = dot_right(low_z, full_z) + dot_right(low_x, full_x) + dot_right(low_dt, full_dt)
    d_normed = sum_pair(part_in, True) + dot_right(low_bc, full_bc)
    d_normed = d_normed.reshape(seq_count, row_count, width)
    grad_gain_in = jnp.sum(d_normed * tokens_f * inv_rms, axis=(0, 1))
    scaled_in = d_normed * gain_in[None, None, :]
    grad_tokens = (
        cotangent.astype(jnp.float32)
        + inv_rms * scaled_in
        - tokens_f * inv_rms**3 * jnp.mean(scaled_in * tokens_f, axis=-1, keepdims=True)
    )
    grad_w_z = dot_left(normed, low_z)
    grad_w_x = dot_left(normed, low_x)
    grad_w_bc = dot_left(normed, low_bc)
    grad_w_dt = dot_left(normed, low_dt)
    small = lax.psum(
        (
            grad_gain_in,
            grad_conv_x,
            grad_conv_bc,
            grad_bias_x,
            grad_bias_bc,
            grad_dt_bias,
            grad_a_log,
            grad_d_skip,
            grad_gain_out,
            grad_w_dt,
        ),
        ("shard", "ctx"),
    )
    owned = reduce_to_owners(
        [part.astype(jnp.bfloat16) for part in (grad_w_out, grad_w_z, grad_w_x, grad_w_bc)]
    )
    units = w_z.shape[1]
    own_out, own_z, own_x, own_bc = (
        owned[:, :units].T,
        owned[:, units : 2 * units],
        owned[:, 2 * units : 3 * units],
        owned[:, 3 * units : 3 * units + bc_units],
    )
    own_rows = w_dt.shape[0]
    own_dt = lax.dynamic_slice_in_dim(
        small[9], lax.axis_index("shard") * own_rows, own_rows, axis=0
    )
    return (
        block_out,
        grad_tokens,
        small[0],
        own_z,
        own_x,
        own_bc,
        own_dt,
        small[1],
        small[2],
        small[3],
        small[4],
        small[5],
        small[6],
        small[7],
        small[8],
        own_out,
    )


def solution(mesh):
    return jax.shard_map(
        shards,
        mesh=mesh,
        in_specs=(
            P("shard", "ctx", None),
            P(),
            P("shard", "tensor"),
            P("shard", "tensor"),
            P("shard", None),
            P("shard", "tensor"),
            P(None, "tensor"),
            P(),
            P("tensor"),
            P(),
            P("tensor"),
            P("tensor"),
            P("tensor"),
            P("tensor"),
            P("tensor", "shard"),
            P("shard", "ctx", None),
        ),
        out_specs=(
            P("shard", "ctx", None),
            P("shard", "ctx", None),
            P(),
            P("shard", "tensor"),
            P("shard", "tensor"),
            P("shard", None),
            P("shard", "tensor"),
            P(None, "tensor"),
            P(),
            P("tensor"),
            P(),
            P("tensor"),
            P("tensor"),
            P("tensor"),
            P("tensor"),
            P("tensor", "shard"),
        ),
        check_vma=False,
    )
```
